512 devices in a mesh: stream: 16 (over z), tile: 4 (over y_lo, core), band: 8 (over y_hi, x).
Axes of the slice: x: 4, y: 4 (y_hi: 2, y_lo: 2; y = y_hi * 2 + y_lo), z: 16, core: 2. Of those that a mesh axis runs over, the one named last changes fastest.
Arguments:
- latents: bfloat16 [384, 8, 512, 256], P('stream', 'band', 'tile'), may hold values from -6 to 6
- owners: int32 [384, 1], P('stream'), may hold values from 0 to 15; in each aligned block of 24 rows (0 to 23, 24 to 47, ...) at most 2 rows name the same one
- live_counts: int32 [16], P('stream'), may hold values from 12 to 24, as said below
- spatial_weight: bfloat16 [3, 3, 256, 256], replicated, may hold values from -0.125 to 0.125
- temporal_weight: bfloat16 [3, 256, 256], replicated, may hold values from -0.21875 to 0.21875
- out_weight: bfloat16 [3, 256], replicated, may hold values from -0.375 to 0.375
Outputs:
- frames: float32 [512, 8, 3, 512], P('stream', 'band', None, 'tile')
The draws below stay inside these ranges and needn't reach their ends.
Inputs may be any that keep to these rules, and one draw needn't show every extreme that they name: `owners`: among the 24 groups of one source device no owner is named more than 2 times, a bound that some block reaches. `live_counts`: some source device has all 24 groups live in every draw.
All inputs are finite; a program needn't handle non-finite values.
Results may differ from the reference program's by a relative error of at most 0.0031.
Values may be sent and summed in bfloat16 or wider, within the bound.
No kernel may reach another device: no remote copies, remote signals or barrier semaphores. Data moves between devices by JAX's collectives and lax.ppermute only.
A program may use at most 128 MiB of HBM per device.

```python
import math
import jax
import jax.numpy as jnp
import numpy as np
from jax import lax

C = 256
SUB = 8
FC = 2
TH = 16
TW = 4
CH = 24
M = 2
CELLS = 128
N_STREAM = 16
N_TILE = 4


def draw_live_counts(key, part):
    key = jax.random.fold_in(key, 11)
    first_key, second_key = jax.random.split(key)
    base_counts = jax.random.randint(first_key, (N_STREAM,), CH // 2, CH + 1)
    chosen = jax.random.randint(second_key, (), 0, N_STREAM)
    positions = jnp.arange(N_STREAM)
    return jnp.where(positions == chosen, CH, base_counts).astype(jnp.int32)


def shard_levels(stream_key, shape, cuts, smallest, high):
    loudness = 1.0
    for axis_at, parts in cuts:
        heights = jax.random.uniform(jax.random.fold_in(jax.random.fold_in(stream_key, 6), axis_at), (parts,), jnp.float32, smallest / len(cuts), high / len(cuts))
        loudness = loudness * jnp.repeat(jnp.exp(heights), shape[axis_at] // parts).reshape((-1,) + (1,) * (len(shape) - 1 - axis_at))
    return loudness


def deal_out(key, own, number, rows, number_of, top, limit, lean):
    order = jax.random.permutation(key, number_of)
    packed, common = portions_of(number_of, rows * top, limit, lean, True), portions_of(number_of, rows * top, limit, lean, False)
    places = jnp.arange(number_of)

    def named(tallies, turn):
        used = int((tallies > 0).sum())
        fixed = max(1, used // 4)
        shifted = fixed + (places - fixed + turn * (used - fixed)) % max(1, number_of - fixed)
        return jnp.zeros((number_of,), jnp.int32).at[order[jnp.where(places < fixed, places, shifted)]].set(jnp.asarray(tallies, jnp.int32))

    tallies = jnp.where(number % 4 == 0, named(packed, number // 4), named(common, number - number // 4 - 1))
    mixed = jax.random.permutation(jax.random.fold_in(own, 3), number_of)
    giver, sink = mixed[0:number_of // 2 * 2:2], mixed[1:number_of // 2 * 2:2]
    margin = jnp.minimum(tallies[giver] - 1, limit - tallies[sink]) // 2
    margin = jnp.where((giver == order[0]) | (sink == order[0]) | (tallies[sink] == 0), 0, jnp.maximum(margin, 0))
    shifted = jax.random.randint(jax.random.fold_in(own, 4), (number_of // 2,), 0, 1 << 20) % (margin + 1)
    tallies = tallies.at[giver].add(-shifted).at[sink].add(shifted)
    labels = jnp.searchsorted(jnp.cumsum(tallies), jnp.arange(rows * top), side="right").astype(jnp.int32)
    grid = labels.reshape(top, rows).T
    grid = grid[jax.random.permutation(jax.random.fold_in(own, 1), rows)]
    turn = jax.random.randint(jax.random.fold_in(own, 2), (rows, 1), 0, top)
    return jnp.take_along_axis(grid, (jnp.arange(top)[None, :] + turn) % top, axis=1)


def portions_of(number_of, total, reach, slope, full):
    portions = [(1 << 20) // math.isqrt(rank ** slope) + 1 for rank in range(1, number_of + 1)]
    largest = reach if full else min(reach, max(-(-total // number_of), total * portions[0] // sum(portions)))
    least = 1 if total - largest >= number_of - 1 else 0
    holding, rest = [largest] + [least] * (number_of - 1), total - largest - least * (number_of - 1)
    while rest > 0:
        candidates = [i for i in range(1, number_of) if holding[i] < largest] or [i for i in range(1, number_of) if holding[i] < reach]
        mass, left = sum([portions[i] for i in candidates]), rest
        for i in candidates:
            extra = min(reach - holding[i], max(1, left * portions[i] // mass), rest)
            holding[i] = holding[i] + extra
            rest = rest - extra
    return np.array(holding)


def bell_draw(rng, shape, spread, limit, shards=(), kind=jnp.bfloat16):
    drawn = jax.random.normal(rng, shape, jnp.float32) * spread
    if len(shards) > 0:
        drawn = shard_levels(rng, shape, shards, -0.22, 0.18) * drawn
    return jnp.clip(drawn, min=-limit, max=limit).astype(kind)


def setup_inputs(seed: int = 0) -> dict:
    streams_of = jax.random.split(jax.random.key(seed), 7)
    latents = bell_draw(streams_of[0], (N_STREAM * CH, SUB, N_TILE * CELLS, C), 1.0, 6.0, ((0, 16), (1, 8), (2, 4)))
    owners_keys = jax.random.split(jax.random.fold_in(streams_of[1], 1), (N_STREAM * CH) // CH)
    owners_turns = jax.random.permutation(jax.random.fold_in(streams_of[1], 3), (N_STREAM * CH) // CH)
    owners = jax.vmap(lambda own, number: deal_out(jax.random.fold_in(streams_of[1], 2), own, number, CH, N_STREAM, 1, M, 2))(owners_keys, owners_turns).reshape((N_STREAM * CH, 1))
    live_counts = draw_live_counts(jax.random.fold_in(streams_of[6], 71), 0)
    spatial_weight = bell_draw(streams_of[3], (3, 3, C, C), (9 * C) ** -0.5, 0.125)
    temporal_weight = bell_draw(streams_of[4], (3, C, C), (3 * C) ** -0.5, 0.21875)
    out_weight = bell_draw(streams_of[5], (3, C), C ** -0.5, 0.375)
    return dict(latents=latents, owners=owners, live_counts=live_counts, spatial_weight=spatial_weight, temporal_weight=temporal_weight, out_weight=out_weight)


def haar_table():
    parity = jnp.arange(8, dtype=jnp.int32)[:, None] & jnp.arange(8, dtype=jnp.int32)[None, :]
    ones_count = (parity & 1) + ((parity >> 1) & 1) + ((parity >> 2) & 1)
    signs = jnp.where(ones_count % 2 == 0, 1.0, -1.0).astype(jnp.float32)
    return signs * jnp.float32(8.0 ** -0.5)


def decode_group(group, spatial_f, temporal_f, out_f, table):
    height = N_TILE * TH
    grid_field = group.reshape(SUB, N_TILE, FC, TH, TW, C).transpose(0, 2, 1, 3, 4, 5)
    grid_field = grid_field.reshape(SUB, FC, height, TW, C).astype(jnp.float32)
    padded = jnp.pad(grid_field, ((0, 0), (0, 0), (1, 1), (1, 1), (0, 0)))
    spatial = jnp.zeros((SUB, FC, height, TW, C), jnp.float32)
    for row_tap in range(3):
        for col_tap in range(3):
            window = padded[:, :, row_tap:row_tap + height, col_tap:col_tap + TW, :]
            spatial = spatial + jnp.einsum("sfhwc,cd->sfhwd", window, spatial_f[row_tap, col_tap])
    activated = lax.optimization_barrier(jax.nn.silu(spatial).astype(jnp.bfloat16)).astype(jnp.float32)
    framed = jnp.pad(activated, ((0, 0), (1, 1), (0, 0), (0, 0), (0, 0)))
    temporal = grid_field
    for time_tap in range(3):
        temporal = temporal + jnp.einsum("sfhwc,cd->sfhwd", framed[:, time_tap:time_tap + FC], temporal_f[time_tap])
    mixed_out = lax.optimization_barrier(temporal.astype(jnp.bfloat16)).astype(jnp.float32)
    pixels = jnp.einsum("oc,sfhwc->sofhw", out_f, mixed_out)
    pixels = pixels.reshape(SUB, 3, FC, N_TILE, TH, TW).transpose(0, 1, 3, 2, 4, 5)
    pixels = pixels.reshape(SUB, 3, N_TILE * FC * TH * TW)
    return jnp.einsum("ps,sok->pok", table, pixels, precision=lax.Precision.HIGHEST)


def reference(latents, owners, live_counts, spatial_weight, temporal_weight, out_weight):
    spatial_f = spatial_weight.astype(jnp.float32)
    temporal_f = temporal_weight.astype(jnp.float32)
    out_f = out_weight.astype(jnp.float32)
    table = haar_table()
    pixel_count = N_TILE * FC * TH * TW
    decoded = lax.map(lambda group: decode_group(group, spatial_f, temporal_f, out_f, table), latents)
    decoded = decoded.reshape(N_STREAM, CH, SUB, 3, pixel_count)
    owner_grid = owners.reshape(N_STREAM, CH).astype(jnp.int32)
    positions = jnp.arange(CH, dtype=jnp.int32)
    same_owner = owner_grid[:, :, None] == owner_grid[:, None, :]
    earlier = positions[:, None] < positions[None, :]
    slot_rank = jnp.sum((same_owner & earlier[None]).astype(jnp.int32), axis=1)
    is_valid = positions[None, :] < live_counts[:, None]
    targets = jnp.arange(N_STREAM * M, dtype=jnp.int32)
    placing = (targets[None, :, None] // M == owner_grid[:, None, :]) & (targets[None, :, None] % M == slot_rank[:, None, :]) & is_valid[:, None, :]
    placed = jnp.einsum("irj,ijpok->ripok", placing.astype(jnp.float32), decoded, precision=lax.Precision.HIGHEST)
    placed = placed.reshape(N_STREAM, M, N_STREAM, SUB, 3, pixel_count).transpose(0, 2, 1, 3, 4, 5)
    return placed.reshape(N_STREAM * N_STREAM * M, SUB, 3, pixel_count)
```

```python
import jax
import jax.numpy as jnp
from jax import lax
from jax.experimental import pallas as pl
from jax.experimental.pallas import tpu as pltpu
from jax.sharding import PartitionSpec as P

C = 256
FC = 2
TH = 16
TW = 4
GB = 8
GF = FC * GB
CELLS = FC * TH * TW
BF = jnp.bfloat16
F32 = jnp.float32


def one_hot_rows(size, order):
    rows = lax.broadcasted_iota(jnp.int32, (size, size), 0)
    cols = lax.broadcasted_iota(jnp.int32, (size, size), 1)
    return (order(rows) == cols).astype(F32).astype(BF)


def dot(a, b):
    return lax.dot_general(a, b, (((1,), (0,)), ((), ())), preferred_element_type=F32)


def silu(x):
    return 0.5 * x * (1.0 + jnp.tanh(0.5 * x))


def decode_kernel(
    even_ref, live_ref, x_ref, side_a_ref, side_b_ref, ws_ref, wt_ref, wo_ref, owners_ref,
    out_ref, xt, perm, perm_side, proj, pix,
):
    step = pl.program_id(0)

    @pl.when(step == 0)
    def _():
        perm[...] = one_hot_rows(
            256, lambda r: (r & 7) * 32 + ((r >> 3) & 1) * 16 + ((r >> 4) & 3) * 4 + (r >> 6)
        )
        perm_side[...] = one_hot_rows(64, lambda r: (r & 7) * 8 + ((r >> 3) & 1) * 4 + (r >> 4))
        wide = jnp.concatenate(
            [jnp.broadcast_to(wo_ref[c : c + 1, :].astype(F32), (CELLS, C)) for c in range(3)], axis=0
        )
        proj[...] = wide.T.astype(BF)

    for part in range(TH // 4):
        rows = jnp.concatenate(
            [x_ref[g, f * 64 + part * 16 : f * 64 + part * 16 + 16, :] for g in range(GB) for f in range(FC)],
            axis=0,
        )
        moved = dot(perm[...], rows).astype(BF)
        for w in range(TW):
            xt[w, 1 + part * 4 : 5 + part * 4] = moved[w * 64 : w * 64 + 64].reshape(4, GF, C)
    even = even_ref[0]
    for side_ref, row in ((side_a_ref, even * 17), (side_b_ref, (1 - even) * 17)):
        moved = dot(perm_side[...], side_ref[...]).astype(BF)
        for w in range(TW):
            xt[w, pl.ds(row, 1)] = moved[w * 16 : w * 16 + 16].reshape(1, GF, C)

    lane = lax.broadcasted_iota(jnp.int32, (GB, CELLS), 1)
    acc = [jnp.zeros((GB, CELLS), F32) for _ in range(3)]
    t_lhs = jnp.concatenate(
        [
            jnp.concatenate([wt_ref[1], wt_ref[0]], axis=1),
            jnp.concatenate([wt_ref[2], wt_ref[1]], axis=1),
        ],
        axis=0,
    )
    for w in range(TW):
        taps = [(dy, dx) for dx in range(3) if 0 <= w + dx - 1 < TW for dy in range(3)]
        lhs = jnp.concatenate([xt[w + dx - 1, dy : dy + TH].reshape(TH * GF, C) for dy, dx in taps], axis=1)
        rhs = jnp.concatenate([ws_ref[dy, dx] for dy, dx in taps], axis=0)
        act = silu(dot(lhs, rhs)).reshape(TH, FC, GB, C)
        frames = [act[:, f].reshape(TH * GB, C).astype(BF) for f in range(FC)]
        temporal = dot(jnp.concatenate(frames, axis=1), t_lhs)
        field = xt[w, 1 : 1 + TH].astype(F32).reshape(TH, FC, GB, C)
        for f in range(FC):
            mixed = (field[:, f].reshape(TH * GB, C) + temporal[:, f * C : (f + 1) * C]).astype(BF)
            pixels = dot(mixed, proj[...])
            for h in range(TH):
                here = lane == f * TH * TW + h * TW + w
                for c in range(3):
                    acc[c] = jnp.where(here, pixels[h * GB : (h + 1) * GB, c * CELLS : (c + 1) * CELLS], acc[c])
    pix[pl.ds(pl.multiple_of(step * GB, GB), GB), :] = jnp.concatenate(acc, axis=1)

    @pl.when(step == pl.num_programs(0) - 1)
    def _():
        count = owners_ref.shape[0]
        slots = out_ref.shape[0]
        slot = lax.broadcasted_iota(jnp.int32, (count, slots), 1)
        group = lax.broadcasted_iota(jnp.int32, (count, slots), 0)
        named = jnp.broadcast_to(owners_ref[...], (count, slots)) == slot // 2
        earlier = (
            lax.broadcasted_iota(jnp.int32, (count, count), 1) < lax.broadcasted_iota(jnp.int32, (count, count), 0)
        )
        rank = dot(earlier.astype(F32).astype(BF), named.astype(F32).astype(BF))
        placed = named & (rank.astype(jnp.int32) == slot % 2) & (group < live_ref[0])
        out_ref[...] = lax.dot_general(
            placed.astype(F32).astype(BF), pix[...].astype(BF), (((0,), (0,)), ((), ())), preferred_element_type=F32
        ).astype(BF)


def decode(even, live, latents, side_a, side_b, ws, wt, wo, owners):
    groups = latents.shape[0]
    slots = 2 * lax.axis_size("stream")
    whole = lambda shape: pl.BlockSpec(shape, lambda b: (0,) * len(shape))
    return pl.pallas_call(
        decode_kernel,
        grid=(groups // GB,),
        out_shape=jax.ShapeDtypeStruct((slots, 3 * CELLS), BF),
        in_specs=[
            pl.BlockSpec(memory_space=pltpu.SMEM),
            pl.BlockSpec(memory_space=pltpu.SMEM),
            pl.BlockSpec((GB, CELLS, C), lambda b: (b, 0, 0)),
            pl.BlockSpec((GB * FC * TW, C), lambda b: (b, 0)),
            pl.BlockSpec((GB * FC * TW, C), lambda b: (b, 0)),
            whole(ws.shape),
            whole(wt.shape),
            whole(wo.shape),
            whole(owners.shape),
        ],
        out_specs=whole((slots, 3 * CELLS)),
        scratch_shapes=[
            pltpu.VMEM((TW, TH + 2, GF, C), BF),
            pltpu.VMEM((256, 256), BF),
            pltpu.VMEM((64, 64), BF),
            pltpu.VMEM((C, 3 * CELLS), BF),
            pltpu.VMEM((groups, 3 * CELLS), F32),
        ],
        compiler_params=pltpu.CompilerParams(vmem_limit_bytes=32 * 1024 * 1024),
        cost_estimate=pl.CostEstimate(flops=5_000_000_000, bytes_accessed=3_500_000, transcendentals=800_000),
        name="decode",
    )(even, live, latents, side_a, side_b, ws, wt, wo, owners)


def local(latents, owners, live_counts, spatial_weight, temporal_weight, out_weight):
    groups = latents.shape[0]
    latents = latents.reshape(groups, CELLS, C)
    field = latents.reshape(groups, FC, TH, TW, C)
    even = 1 - lax.axis_index("tile") % 2
    head = field[:, :, 0].reshape(groups * FC * TW, C)
    tail = field[:, :, TH - 1].reshape(groups * FC * TW, C)
    send_a = jnp.where(even == 1, tail, head)
    send_b = jnp.where(even == 1, head, tail)
    side_b = lax.ppermute(send_b, "tile", [(1, 2), (2, 1)])
    side_a = lax.ppermute(send_a, "tile", [(0, 1), (1, 0), (2, 3), (3, 2)])
    placed = decode(
        even.reshape(1), live_counts, latents, side_a, side_b, spatial_weight, temporal_weight, out_weight, owners
    )
    streams, bands = lax.axis_size("stream"), lax.axis_size("band")
    outgoing = jnp.broadcast_to(placed.reshape(1, streams, 2, 3 * CELLS), (bands, streams, 2, 3 * CELLS))
    got = lax.all_to_all(
        outgoing.reshape(bands * streams, 2, 3 * CELLS), ("band", "stream"), split_axis=0, concat_axis=0, tiled=True
    )
    parity = lax.axis_index("band")
    signs = 1 - 2 * (lax.population_count(parity & jnp.arange(bands, dtype=jnp.int32)) & 1)
    got = got.reshape(bands, streams * 2, 3, CELLS).astype(F32)
    frames = jnp.sum(got * signs.astype(F32)[:, None, None, None], axis=0) * F32(8.0**-0.5)
    return frames.reshape(streams * 2, 1, 3, CELLS)


def solution(mesh):
    return jax.shard_map(
        local,
        mesh=mesh,
        in_specs=(P("stream", "band", "tile", None), P("stream", None), P("stream"), P(), P(), P()),
        out_specs=P("stream", "band", None, "tile"),
        check_vma=False,
    )
```

```python
import jax
import jax.numpy as jnp
from jax import lax
from jax.experimental import pallas as pl
from jax.experimental.pallas import tpu as pltpu
from jax.sharding import PartitionSpec as P

C = 256
FC = 2
TH = 16
TW = 4
GB = 8
GF = FC * GB
CELLS = FC * TH * TW
HALF = TH * TW
BF = jnp.bfloat16
F32 = jnp.float32


def dot(a, b):
    return lax.dot_general(a, b, (((1,), (0,)), ((), ())), preferred_element_type=F32)


def silu(x):
    return 0.5 * x * (1.0 + jnp.tanh(0.5 * x))


def one_hot(rows, cols, place):
    row = lax.broadcasted_iota(jnp.int32, (rows, cols), 0)
    col = lax.broadcasted_iota(jnp.int32, (rows, cols), 1)
    return (place(row) == col).astype(F32).astype(BF)


def temporal_matrix(wt_ref):
    first = jnp.concatenate([wt_ref[1], wt_ref[0]], axis=1)
    second = jnp.concatenate([wt_ref[2], wt_ref[1]], axis=1)
    return jnp.concatenate([first, second], axis=0)


def edges_kernel(even_ref, x_ref, a_ref, b_ref, slab, sems):
    even = even_ref[0]
    blocks = x_ref.shape[0] // GB
    copies = []
    for side in range(2):
        last = even if side == 0 else 1 - even
        for f in range(FC):
            start = pl.multiple_of(f * HALF + last * (HALF - 8), 8)
            copies.append(
                pltpu.make_async_copy(x_ref.at[:, pl.ds(start, 8), :], slab.at[side, f], sems.at[side, f])
            )
    for copy in copies:
        copy.start()
    for side, out_ref in enumerate((a_ref, b_ref)):
        last = even if side == 0 else 1 - even
        pick = one_hot(
            TW * GF, FC * GB * 8, lambda r: ((r >> 3) & 1) * (GB * 8) + (r & 7) * 8 + last * 4 + (r >> 4)
        )
        for f in range(FC):
            copies[side * FC + f].wait()
        for b in range(blocks):
            rows = slab[side, :, b * GB : (b + 1) * GB].reshape(FC * GB * 8, C)
            moved = dot(pick, rows).astype(BF)
            for w in range(TW):
                at = (w * blocks + b) * GF
                out_ref[at : at + GF, :] = moved[w * GF : (w + 1) * GF]


def edges(even, latents):
    groups = latents.shape[0]
    side = jax.ShapeDtypeStruct((TW * groups * FC, C), BF)
    vmem = pl.BlockSpec(memory_space=pltpu.VMEM)
    return pl.pallas_call(
        edges_kernel,
        out_shape=(side, side),
        in_specs=[pl.BlockSpec(memory_space=pltpu.SMEM), pl.BlockSpec(memory_space=pltpu.HBM)],
        out_specs=(vmem, vmem),
        scratch_shapes=[pltpu.VMEM((2, FC, groups, 8, C), BF), pltpu.SemaphoreType.DMA((2, FC))],
        cost_estimate=pl.CostEstimate(flops=50_000_000, bytes_accessed=800_000, transcendentals=0),
        name="edges",
    )(even, latents)


def main_kernel(x_ref, ws_ref, wt_ref, wo_ref, rim_ref, field_ref, sums_ref, proj_ref, xt, act, mix):
    blocks = x_ref.shape[0] // GB
    width = blocks * GF
    half = blocks * GB
    perm = one_hot(256, 256, lambda r: (r & 7) * 32 + ((r >> 3) & 1) * 16 + ((r >> 4) & 3) * 4 + (r >> 6))
    wide = [jnp.broadcast_to(wo_ref[min(c, 2) : min(c, 2) + 1, :].astype(F32), (HALF, C)) for c in range(4)]
    proj_ref[...] = jnp.concatenate(wide, axis=0).T.astype(BF)
    zero_row = jnp.zeros((width, C), BF)
    for w in range(TW):
        xt[w, 0] = zero_row
        xt[w, TH + 1] = zero_row
    for b in range(blocks):
        for part in range(TH // 4):
            rows = jnp.concatenate(
                [
                    x_ref[b * GB + g, f * HALF + part * 16 : f * HALF + part * 16 + 16, :]
                    for g in range(GB)
                    for f in range(FC)
                ],
                axis=0,
            )
            moved = dot(perm, rows).astype(BF)
            for w in range(TW):
                xt[w, 1 + part * 4 : 5 + part * 4, b * GF : (b + 1) * GF] = moved[w * 64 : w * 64 + 64].reshape(4, GF, C)
    inner = TH - 2
    for w in range(TW):
        taps = [(dy, dx) for dx in range(3) if 0 <= w + dx - 1 < TW for dy in range(3)]
        lhs = jnp.concatenate([xt[w + dx - 1, dy : dy + TH].reshape(TH * width, C) for dy, dx in taps], axis=1)
        rhs = jnp.concatenate([ws_ref[dy, dx] for dy, dx in taps], axis=0)
        total = dot(lhs, rhs).reshape(TH, width, C)
        rim_ref[0, w] = total[0]
        rim_ref[1, w] = total[TH - 1]
        field_ref[0, w] = xt[w, 1]
        field_ref[1, w] = xt[w, TH]
        live = silu(total[1 : TH - 1].reshape(inner * width, C)).reshape(inner * blocks, FC, GB, C)
        for f in range(FC):
            act[w, :, f * C : (f + 1) * C] = live[:, f].reshape(inner * half, C).astype(BF)
    for w in range(TW):
        temporal = dot(act[w], temporal_matrix(wt_ref))
        field = xt[w, 2:TH].astype(F32).reshape(inner * blocks, FC, GB, C)
        for f in range(FC):
            mix[w, f] = (field[:, f].reshape(inner * half, C) + temporal[:, f * C : (f + 1) * C]).astype(BF)
    lane = lax.broadcasted_iota(jnp.int32, (GB, 4 * HALF), 1) & (HALF - 1)
    sums = [[jnp.zeros((GB, 4 * HALF), F32) for _ in range(FC)] for _ in range(blocks)]
    for w in range(TW):
        for f in range(FC):
            pixels = dot(mix[w, f], proj_ref[...])
            for h in range(inner):
                here = lane == (h + 1) * TW + w
                for b in range(blocks):
                    at = (h * blocks + b) * GB
                    sums[b][f] = jnp.where(here, pixels[at : at + GB], sums[b][f])
    for b in range(blocks):
        for f in range(FC):
            sums_ref[b, f] = sums[b][f]


def main(latents, ws, wt, wo):
    groups = latents.shape[0]
    width = groups * FC
    vmem = pl.BlockSpec(memory_space=pltpu.VMEM)
    return pl.pallas_call(
        main_kernel,
        out_shape=(
            jax.ShapeDtypeStruct((2, TW, width, C), F32),
            jax.ShapeDtypeStruct((2, TW, width, C), BF),
            jax.ShapeDtypeStruct((groups // GB, FC, GB, 4 * HALF), F32),
            jax.ShapeDtypeStruct((C, 4 * HALF), BF),
        ),
        in_specs=[vmem] * 4,
        out_specs=(vmem,) * 4,
        scratch_shapes=[
            pltpu.VMEM((TW, TH + 2, width, C), BF),
            pltpu.VMEM((TW, (TH - 2) * groups, FC * C), BF),
            pltpu.VMEM((TW, FC, (TH - 2) * groups, C), BF),
        ],
        compiler_params=pltpu.CompilerParams(vmem_limit_bytes=32 * 1024 * 1024),
        cost_estimate=pl.CostEstimate(flops=5_000_000_000, bytes_accessed=4_500_000, transcendentals=700_000),
        name="main",
    )(latents, ws, wt, wo)


def finish_kernel(
    even_ref, live_ref, a_ref, b_ref, rim_ref, field_ref, sums_ref, proj_ref, ws_ref, wt_ref, owners_ref, out_ref
):
    blocks = sums_ref.shape[0]
    count = blocks * GB
    width = count * FC
    even = even_ref[0] == 1
    top = jnp.where(even, b_ref[...], a_ref[...])
    bottom = jnp.where(even, a_ref[...], b_ref[...])
    acts = []
    for side, (halo, dy) in enumerate(((top, 0), (bottom, 2))):
        total = rim_ref[side].reshape(TW * width, C) + dot(halo, ws_ref[dy, 1])
        left = dot(halo[: (TW - 1) * width], ws_ref[dy, 0])
        right = dot(halo[width:], ws_ref[dy, 2])
        gap = jnp.zeros((width, C), F32)
        total = total + jnp.concatenate([gap, left], axis=0) + jnp.concatenate([right, gap], axis=0)
        acts.append(silu(total).reshape(TW * blocks, FC, GB, C))
    frames = [
        jnp.concatenate([acts[side][:, f].reshape(TW * count, C) for side in range(2)], axis=0).astype(BF)
        for f in range(FC)
    ]
    temporal = dot(jnp.concatenate(frames, axis=1), temporal_matrix(wt_ref))
    field = field_ref[...].astype(F32).reshape(2 * TW * blocks, FC, GB, C)
    lane = lax.broadcasted_iota(jnp.int32, (GB, 4 * HALF), 1) & (HALF - 1)
    narrow = lax.broadcasted_iota(jnp.int32, (GB, CELLS), 1) < HALF
    sums = [[sums_ref[b, f] for f in range(FC)] for b in range(blocks)]
    for f in range(FC):
        mixed = (field[:, f].reshape(2 * TW * count, C) + temporal[:, f * C : (f + 1) * C]).astype(BF)
        pixels = dot(mixed, proj_ref[...])
        for side, h in ((0, 0), (1, TH - 1)):
            for w in range(TW):
                here = lane == h * TW + w
                for b in range(blocks):
                    at = ((side * TW + w) * blocks + b) * GB
                    sums[b][f] = jnp.where(here, pixels[at : at + GB], sums[b][f])
    channels = []
    for c in range(3):
        at = c // 2 * CELLS
        for b in range(blocks):
            first, second = sums[b][0][:, at : at + CELLS], sums[b][1][:, at : at + CELLS]
            if c % 2 == 0:
                second = pltpu.roll(second, HALF, 1)
            else:
                first = pltpu.roll(first, HALF, 1)
            channels.append(jnp.where(narrow, first, second))
    stacked = jnp.concatenate(channels, axis=0).astype(BF)
    slots = out_ref.shape[0] // 8
    row = lax.broadcasted_iota(jnp.int32, (slots, count), 0) // 3
    group = lax.broadcasted_iota(jnp.int32, (slots, count), 1)
    named = jnp.broadcast_to(owners_ref[...], (slots, count)) == row // 2
    earlier = lax.broadcasted_iota(jnp.int32, (count, count), 0) < lax.broadcasted_iota(jnp.int32, (count, count), 1)
    rank = dot(named.astype(F32).astype(BF), earlier.astype(F32).astype(BF)).astype(jnp.int32)
    placed = named & (rank == row % 2) & (group < live_ref[0])
    channel = lax.broadcasted_iota(jnp.int32, (slots, count), 0) % 3
    placing = jnp.concatenate([(placed & (channel == c)).astype(F32) for c in range(3)], axis=1).astype(BF)
    message = dot(placing, stacked).astype(BF)
    for p in range(8):
        out_ref[p * slots : (p + 1) * slots, :] = message


def finish(even, live, side_a, side_b, rim, field, sums, proj, ws, wt, owners, rows):
    vmem = pl.BlockSpec(memory_space=pltpu.VMEM)
    smem = pl.BlockSpec(memory_space=pltpu.SMEM)
    return pl.pallas_call(
        finish_kernel,
        out_shape=jax.ShapeDtypeStruct((rows, CELLS), BF),
        in_specs=[smem, smem] + [vmem] * 9,
        out_specs=vmem,
        compiler_params=pltpu.CompilerParams(vmem_limit_bytes=32 * 1024 * 1024),
        cost_estimate=pl.CostEstimate(flops=500_000_000, bytes_accessed=3_000_000, transcendentals=100_000),
        name="finish",
    )(even, live, side_a, side_b, rim, field, sums, proj, ws, wt, owners)


def local(latents, owners, live_counts, spatial_weight, temporal_weight, out_weight):
    groups = latents.shape[0]
    latents = latents.reshape(groups, CELLS, C)
    streams, bands = lax.axis_size("stream"), lax.axis_size("band")
    even = (1 - (lax.axis_index("tile") & 1)).reshape(1)
    send_a, send_b = edges(even, latents)
    side_b = lax.ppermute(send_b, "tile", [(1, 2), (2, 1)])
    side_a = lax.ppermute(send_a, "tile", [(0, 1), (1, 0), (2, 3), (3, 2)])
    rim, field, sums, proj = main(latents, spatial_weight, temporal_weight, out_weight)
    rows = bands * streams * 2 * 3
    outgoing = finish(
        even, live_counts, side_a, side_b, rim, field, sums, proj, spatial_weight, temporal_weight,
        owners.reshape(1, groups), rows,
    )
    parity = lax.axis_index("band")
    signs = 1 - 2 * (lax.population_count(parity & jnp.arange(bands, dtype=jnp.int32)) & 1)
    signs = signs.astype(F32) * F32(8.0**-0.5)
    outgoing, signs = lax.optimization_barrier((outgoing.reshape(rows // 2, 2, CELLS), signs))
    got = lax.all_to_all(outgoing, ("band", "stream"), split_axis=0, concat_axis=0, tiled=True)
    got = got.reshape(bands, streams * 2 * 3, CELLS).astype(F32)
    frames = jnp.sum(got * signs[:, None, None], axis=0)
    return frames.reshape(streams * 2, 1, 3, CELLS)


def solution(mesh):
    return jax.shard_map(
        local,
        mesh=mesh,
        in_specs=(P("stream", "band", "tile", None), P("stream", None), P("stream"), P(), P(), P()),
        out_specs=P("stream", "band", None, "tile"),
        check_vma=False,
    )
```

```python
import jax
import jax.numpy as jnp
from jax import lax
from jax.experimental import pallas as pl
from jax.experimental.pallas import tpu as pltpu
from jax.sharding import PartitionSpec as P

C = 256
FC = 2
TH = 16
TW = 4
GB = 8
GF = FC * GB
CELLS = FC * TH * TW
HALF = TH * TW
BF = jnp.bfloat16
F32 = jnp.float32


def dot(a, b):
    return lax.dot_general(a, b, (((1,), (0,)), ((), ())), preferred_element_type=F32)


def silu(x):
    return 0.5 * x * (1.0 + jnp.tanh(0.5 * x))


def one_hot(rows, cols, place):
    row = lax.broadcasted_iota(jnp.int32, (rows, cols), 0)
    col = lax.broadcasted_iota(jnp.int32, (rows, cols), 1)
    return (place(row) == col).astype(F32).astype(BF)


def temporal_matrix(wt_ref):
    first = jnp.concatenate([wt_ref[1], wt_ref[0]], axis=1)
    second = jnp.concatenate([wt_ref[2], wt_ref[1]], axis=1)
    return jnp.concatenate([first, second], axis=0)


def prep_kernel(
    even_ref, x_ref, ws_ref, wo_ref, a_ref, b_ref, xt_ref, ws_out, proj_ref, slab, wo_buf, sems
):
    groups = x_ref.shape[0]
    blocks = groups // GB
    width = blocks * GF
    x_copies = [
        pltpu.make_async_copy(x_ref.at[b * GB : (b + 1) * GB], slab.at[b * GB : (b + 1) * GB], sems.at[b])
        for b in range(blocks)
    ]
    wo_copy = pltpu.make_async_copy(wo_ref, wo_buf, sems.at[blocks])
    ws_copy = pltpu.make_async_copy(ws_ref, ws_out, sems.at[blocks + 1])
    for copy in [wo_copy] + x_copies + [ws_copy]:
        copy.start()
    perm = one_hot(256, 256, lambda r: (r & 7) * 32 + ((r >> 3) & 1) * 16 + ((r >> 4) & 3) * 4 + (r >> 6))
    zero_row = jnp.zeros((width, C), BF)
    for w in range(TW):
        xt_ref[w, 0] = zero_row
        xt_ref[w, TH + 1] = zero_row
    wo_copy.wait()
    wide = [jnp.broadcast_to(wo_buf[min(c, 2) : min(c, 2) + 1, :].astype(F32), (HALF, C)) for c in range(4)]
    proj_ref[...] = jnp.concatenate(wide, axis=0).T.astype(BF)
    for b in range(blocks):
        x_copies[b].wait()
        for part in range(TH // 4):
            rows = jnp.concatenate(
                [
                    slab[b * GB + g, f * HALF + part * 16 : f * HALF + part * 16 + 16, :]
                    for g in range(GB)
                    for f in range(FC)
                ],
                axis=0,
            )
            moved = dot(perm, rows).astype(BF)
            for w in range(TW):
                xt_ref[w, 1 + part * 4 : 5 + part * 4, b * GF : (b + 1) * GF] = moved[w * 64 : w * 64 + 64].reshape(
                    4, GF, C
                )
    even = even_ref[0]
    for out_ref, row in ((a_ref, 1 + even * (TH - 1)), (b_ref, TH - even * (TH - 1))):
        for w in range(TW):
            out_ref[w * width : (w + 1) * width, :] = xt_ref[w, row]
    ws_copy.wait()


def prep(even, latents, ws, wo):
    groups = latents.shape[0]
    width = groups * FC
    vmem = pl.BlockSpec(memory_space=pltpu.VMEM)
    hbm = pl.BlockSpec(memory_space=pltpu.HBM)
    return pl.pallas_call(
        prep_kernel,
        out_shape=(
            jax.ShapeDtypeStruct((TW * width, C), BF),
            jax.ShapeDtypeStruct((TW * width, C), BF),
            jax.ShapeDtypeStruct((TW, TH + 2, width, C), BF),
            jax.ShapeDtypeStruct(ws.shape, BF),
            jax.ShapeDtypeStruct((C, 4 * HALF), BF),
        ),
        in_specs=[pl.BlockSpec(memory_space=pltpu.SMEM)] + [hbm] * 3,
        out_specs=(vmem,) * 5,
        scratch_shapes=[
            pltpu.VMEM(latents.shape, BF),
            pltpu.VMEM(wo.shape, BF),
            pltpu.SemaphoreType.DMA((groups // GB + 2,)),
        ],
        compiler_params=pltpu.CompilerParams(vmem_limit_bytes=32 * 1024 * 1024),
        cost_estimate=pl.CostEstimate(flops=400_000_000, bytes_accessed=3_200_000, transcendentals=0),
        name="prep",
    )(even, *(pltpu.with_memory_space_constraint(a, pltpu.HBM) for a in (latents, ws, wo)))


def main_kernel(xt, ws_ref, wt_hbm, proj_ref, rim_ref, field_ref, sums_ref, wt_ref, act, mix, sem):
    wt_copy = pltpu.make_async_copy(wt_hbm, wt_ref, sem)
    wt_copy.start()
    width = xt.shape[2]
    blocks = width // GF
    half = blocks * GB
    inner = TH - 2
    for w in range(TW):
        taps = [(dy, dx) for dx in range(3) if 0 <= w + dx - 1 < TW for dy in range(3)]
        lhs = jnp.concatenate([xt[w + dx - 1, dy : dy + TH].reshape(TH * width, C) for dy, dx in taps], axis=1)
        rhs = jnp.concatenate([ws_ref[dy, dx] for dy, dx in taps], axis=0)
        total = dot(lhs, rhs).reshape(TH, width, C)
        rim_ref[0, w] = total[0]
        rim_ref[1, w] = total[TH - 1]
        field_ref[0, w] = xt[w, 1]
        field_ref[1, w] = xt[w, TH]
        live = silu(total[1 : TH - 1].reshape(inner * width, C)).reshape(inner * blocks, FC, GB, C)
        for f in range(FC):
            act[w, :, f * C : (f + 1) * C] = live[:, f].reshape(inner * half, C).astype(BF)
    wt_copy.wait()
    for w in range(TW):
        temporal = dot(act[w], temporal_matrix(wt_ref))
        field = xt[w, 2:TH].astype(F32).reshape(inner * blocks, FC, GB, C)
        for f in range(FC):
            mix[w, f] = (field[:, f].reshape(inner * half, C) + temporal[:, f * C : (f + 1) * C]).astype(BF)
    lane = lax.broadcasted_iota(jnp.int32, (GB, 4 * HALF), 1) & (HALF - 1)
    sums = [[jnp.zeros((GB, 4 * HALF), F32) for _ in range(FC)] for _ in range(blocks)]
    for w in range(TW):
        for f in range(FC):
            pixels = dot(mix[w, f], proj_ref[...])
            for h in range(inner):
                here = lane == (h + 1) * TW + w
                for b in range(blocks):
                    at = (h * blocks + b) * GB
                    sums[b][f] = jnp.where(here, pixels[at : at + GB], sums[b][f])
    for b in range(blocks):
        for f in range(FC):
            sums_ref[b, f] = sums[b][f]


def main(xt, ws, wt, proj):
    width = xt.shape[2]
    groups = width // FC
    vmem = pl.BlockSpec(memory_space=pltpu.VMEM)
    return pl.pallas_call(
        main_kernel,
        out_shape=(
            jax.ShapeDtypeStruct((2, TW, width, C), F32),
            jax.ShapeDtypeStruct((2, TW, width, C), BF),
            jax.ShapeDtypeStruct((groups // GB, FC, GB, 4 * HALF), F32),
            jax.ShapeDtypeStruct(wt.shape, BF),
        ),
        in_specs=[vmem, vmem, pl.BlockSpec(memory_space=pltpu.HBM), vmem],
        out_specs=(vmem,) * 4,
        scratch_shapes=[
            pltpu.VMEM((TW, (TH - 2) * groups, FC * C), BF),
            pltpu.VMEM((TW, FC, (TH - 2) * groups, C), BF),
            pltpu.SemaphoreType.DMA,
        ],
        compiler_params=pltpu.CompilerParams(vmem_limit_bytes=32 * 1024 * 1024),
        cost_estimate=pl.CostEstimate(flops=4_500_000_000, bytes_accessed=4_500_000, transcendentals=700_000),
        name="main",
    )(xt, ws, pltpu.with_memory_space_constraint(wt, pltpu.HBM), proj)


def finish_kernel(
    even_ref, live_ref, a_ref, b_ref, rim_ref, field_ref, sums_ref, proj_ref, ws_ref, wt_ref, owners_ref, out_ref
):
    blocks = sums_ref.shape[0]
    count = blocks * GB
    width = count * FC
    even = even_ref[0] == 1
    top = jnp.where(even, b_ref[...], a_ref[...])
    bottom = jnp.where(even, a_ref[...], b_ref[...])
    acts = []
    for side, (halo, dy) in enumerate(((top, 0), (bottom, 2))):
        total = rim_ref[side].reshape(TW * width, C) + dot(halo, ws_ref[dy, 1])
        left = dot(halo[: (TW - 1) * width], ws_ref[dy, 0])
        right = dot(halo[width:], ws_ref[dy, 2])
        gap = jnp.zeros((width, C), F32)
        total = total + jnp.concatenate([gap, left], axis=0) + jnp.concatenate([right, gap], axis=0)
        acts.append(silu(total).reshape(TW * blocks, FC, GB, C))
    frames = [
        jnp.concatenate([acts[side][:, f].reshape(TW * count, C) for side in range(2)], axis=0).astype(BF)
        for f in range(FC)
    ]
    temporal = dot(jnp.concatenate(frames, axis=1), temporal_matrix(wt_ref))
    field = field_ref[...].astype(F32).reshape(2 * TW * blocks, FC, GB, C)
    lane = lax.broadcasted_iota(jnp.int32, (GB, 4 * HALF), 1) & (HALF - 1)
    narrow = lax.broadcasted_iota(jnp.int32, (GB, CELLS), 1) < HALF
    sums = [[sums_ref[b, f] for f in range(FC)] for b in range(blocks)]
    for f in range(FC):
        mixed = (field[:, f].reshape(2 * TW * count, C) + temporal[:, f * C : (f + 1) * C]).astype(BF)
        pixels = dot(mixed, proj_ref[...])
        for side, h in ((0, 0), (1, TH - 1)):
            for w in range(TW):
                here = lane == h * TW + w
                for b in range(blocks):
                    at = ((side * TW + w) * blocks + b) * GB
                    sums[b][f] = jnp.where(here, pixels[at : at + GB], sums[b][f])
    channels = []
    for c in range(3):
        at = c // 2 * CELLS
        for b in range(blocks):
            first, second = sums[b][0][:, at : at + CELLS], sums[b][1][:, at : at + CELLS]
            if c % 2 == 0:
                second = pltpu.roll(second, HALF, 1)
            else:
                first = pltpu.roll(first, HALF, 1)
            channels.append(jnp.where(narrow, first, second))
    stacked = jnp.concatenate(channels, axis=0).astype(BF)
    slots = out_ref.shape[0] // 8
    row = lax.broadcasted_iota(jnp.int32, (slots, count), 0) // 3
    group = lax.broadcasted_iota(jnp.int32, (slots, count), 1)
    streams = slots // 6
    named = jnp.broadcast_to(owners_ref[...], (slots, count)) == (row // 2 + streams // 2) % streams
    earlier = lax.broadcasted_iota(jnp.int32, (count, count), 0) < lax.broadcasted_iota(jnp.int32, (count, count), 1)
    rank = dot(named.astype(F32).astype(BF), earlier.astype(F32).astype(BF)).astype(jnp.int32)
    placed = named & (rank == row % 2) & (group < live_ref[0])
    channel = lax.broadcasted_iota(jnp.int32, (slots, count), 0) % 3
    placing = jnp.concatenate([(placed & (channel == c)).astype(F32) for c in range(3)], axis=1).astype(BF)
    message = dot(placing, stacked).astype(BF)
    for p in range(8):
        out_ref[p * slots : (p + 1) * slots, :] = message


def finish(even, live, side_a, side_b, rim, field, sums, proj, ws, wt, owners, rows):
    vmem = pl.BlockSpec(memory_space=pltpu.VMEM)
    smem = pl.BlockSpec(memory_space=pltpu.SMEM)
    return pl.pallas_call(
        finish_kernel,
        out_shape=jax.ShapeDtypeStruct((rows, CELLS), BF),
        in_specs=[smem, smem] + [vmem] * 9,
        out_specs=vmem,
        compiler_params=pltpu.CompilerParams(vmem_limit_bytes=32 * 1024 * 1024),
        cost_estimate=pl.CostEstimate(flops=500_000_000, bytes_accessed=3_000_000, transcendentals=100_000),
        name="finish",
    )(even, live, side_a, side_b, rim, field, sums, proj, ws, wt, owners)


def local(latents, owners, live_counts, spatial_weight, temporal_weight, out_weight):
    groups = latents.shape[0]
    latents = latents.reshape(groups, CELLS, C)
    streams, bands = lax.axis_size("stream"), lax.axis_size("band")
    even = (1 - (lax.axis_index("tile") & 1)).reshape(1)
    send_a, send_b, xt, ws, proj = prep(even, latents, spatial_weight, out_weight)
    side_b = lax.ppermute(send_b, "tile", [(1, 2), (2, 1)])
    side_a = lax.ppermute(send_a, "tile", [(0, 1), (1, 0), (2, 3), (3, 2)])
    rim, field, sums, wt = main(xt, ws, temporal_weight, proj)
    rows = bands * streams * 2 * 3
    outgoing = finish(even, live_counts, side_a, side_b, rim, field, sums, proj, ws, wt, owners.reshape(1, groups), rows)
    band_list = list(range(bands))[::-1]
    stream_list = list(range(streams // 2, streams)) + list(range(streams // 2))
    parity = lax.axis_index("band")
    signs = 1 - 2 * (lax.population_count(parity & (bands - 1 - jnp.arange(bands, dtype=jnp.int32))) & 1)
    signs = signs.astype(F32) * F32(8.0**-0.5)
    outgoing, signs = lax.optimization_barrier((outgoing.reshape(bands, streams * 6, CELLS), signs))
    got = lax.all_to_all(
        outgoing, "band", split_axis=0, concat_axis=0, tiled=True, axis_index_groups=[band_list]
    )
    frames = jnp.sum(got.astype(F32) * signs[:, None, None], axis=0)
    frames = lax.optimization_barrier(frames.reshape(streams * 3, 2, CELLS))
    frames = lax.all_to_all(
        frames, "stream", split_axis=0, concat_axis=0, tiled=True, axis_index_groups=[stream_list]
    )
    frames = jnp.roll(frames.reshape(streams, 6, CELLS), streams // 2, axis=0)
    return frames.reshape(streams * 2, 1, 3, CELLS)


def solution(mesh):
    return jax.shard_map(
        local,
        mesh=mesh,
        in_specs=(P("stream", "band", "tile", None), P("stream", None), P("stream"), P(), P(), P()),
        out_specs=P("stream", "band", None, "tile"),
        check_vma=False,
    )
```

```python
import jax
import jax.numpy as jnp
from jax import lax
from jax.experimental import pallas as pl
from jax.experimental.pallas import tpu as pltpu
from jax.sharding import PartitionSpec as P

C = 256
FC = 2
TH = 16
TW = 4
GB = 8
GF = FC * GB
CELLS = FC * TH * TW
HALF = TH * TW
BF = jnp.bfloat16
F32 = jnp.float32


def dot(a, b):
    return lax.dot_general(a, b, (((1,), (0,)), ((), ())), preferred_element_type=F32)


def silu(x):
    return 0.5 * x * (1.0 + jnp.tanh(0.5 * x))


def one_hot(rows, cols, place):
    wanted = jnp.broadcast_to(place(lax.broadcasted_iota(jnp.int32, (rows, 1), 0)), (rows, cols))
    return jnp.where(wanted == lax.broadcasted_iota(jnp.int32, (rows, cols), 1), 1.0, 0.0).astype(BF)


def temporal_matrix(wt_ref):
    first = jnp.concatenate([wt_ref[1], wt_ref[0]], axis=1)
    second = jnp.concatenate([wt_ref[2], wt_ref[1]], axis=1)
    return jnp.concatenate([first, second], axis=0)


def prep_kernel(
    even_ref, x_ref, ws_ref, a_ref, b_ref, xt_ref, ws_out, slab, sems
):
    groups = x_ref.shape[0]
    blocks = groups // GB
    width = blocks * GF
    x_copies = [
        pltpu.make_async_copy(x_ref.at[b * GB : (b + 1) * GB], slab.at[b * GB : (b + 1) * GB], sems.at[b])
        for b in range(blocks)
    ]
    ws_copy = pltpu.make_async_copy(ws_ref, ws_out, sems.at[blocks])
    for copy in x_copies + [ws_copy]:
        copy.start()
    perm = one_hot(256, 256, lambda r: (r & 7) * 32 + ((r >> 3) & 1) * 16 + ((r >> 4) & 3) * 4 + (r >> 6))
    zero_row = jnp.zeros((width, C), BF)
    for w in range(TW):
        xt_ref[w, 0] = zero_row
        xt_ref[w, TH + 1] = zero_row
    for b in range(blocks):
        x_copies[b].wait()
        for part in range(TH // 4):
            rows = jnp.concatenate(
                [
                    slab[b * GB + g, f * HALF + part * 16 : f * HALF + part * 16 + 16, :]
                    for g in range(GB)
                    for f in range(FC)
                ],
                axis=0,
            )
            moved = dot(perm, rows).astype(BF)
            for w in range(TW):
                xt_ref[w, 1 + part * 4 : 5 + part * 4, b * GF : (b + 1) * GF] = moved[w * 64 : w * 64 + 64].reshape(
                    4, GF, C
                )
    even = even_ref[0]
    for out_ref, row in ((a_ref, 1 + even * (TH - 1)), (b_ref, TH - even * (TH - 1))):
        for w in range(TW):
            out_ref[w * width : (w + 1) * width, :] = xt_ref[w, row]
    ws_copy.wait()


def prep(even, latents, ws):
    groups = latents.shape[0]
    width = groups * FC
    vmem = pl.BlockSpec(memory_space=pltpu.VMEM)
    hbm = pl.BlockSpec(memory_space=pltpu.HBM)
    return pl.pallas_call(
        prep_kernel,
        out_shape=(
            jax.ShapeDtypeStruct((TW * width, C), BF),
            jax.ShapeDtypeStruct((TW * width, C), BF),
            jax.ShapeDtypeStruct((TW, TH + 2, width, C), BF),
            jax.ShapeDtypeStruct(ws.shape, BF),
        ),
        in_specs=[pl.BlockSpec(memory_space=pltpu.SMEM)] + [hbm] * 2,
        out_specs=(vmem,) * 4,
        scratch_shapes=[
            pltpu.VMEM(latents.shape, BF),
            pltpu.SemaphoreType.DMA((groups // GB + 1,)),
        ],
        compiler_params=pltpu.CompilerParams(vmem_limit_bytes=32 * 1024 * 1024),
        cost_estimate=pl.CostEstimate(flops=400_000_000, bytes_accessed=3_200_000, transcendentals=0),
        name="prep",
    )(even, *(pltpu.with_memory_space_constraint(a, pltpu.HBM) for a in (latents, ws)))


def main_kernel(xt, ws_ref, wt_hbm, wo_ref, rim_ref, field_ref, sums_ref, wt_ref, proj_ref, act, mix, sem):
    wt_copy = pltpu.make_async_copy(wt_hbm, wt_ref, sem)
    wt_copy.start()
    channel = lax.broadcasted_iota(jnp.int32, (wo_ref.shape[0], 4 * HALF), 1) // HALF
    spread = (channel == lax.broadcasted_iota(jnp.int32, channel.shape, 0)).astype(F32)
    proj_ref[...] = lax.dot_general(
        wo_ref[...].astype(F32), spread, (((0,), (0,)), ((), ())), preferred_element_type=F32
    ).astype(BF)
    width = xt.shape[2]
    blocks = width // GF
    half = blocks * GB
    inner = TH - 2
    for w in range(TW):
        taps = [(dy, dx) for dx in range(3) if 0 <= w + dx - 1 < TW for dy in range(3)]
        lhs = jnp.concatenate([xt[w + dx - 1, dy : dy + TH].reshape(TH * width, C) for dy, dx in taps], axis=1)
        rhs = jnp.concatenate([ws_ref[dy, dx] for dy, dx in taps], axis=0)
        total = dot(lhs, rhs).reshape(TH, width, C)
        rim_ref[0, w] = total[0]
        rim_ref[1, w] = total[TH - 1]
        field_ref[0, w] = xt[w, 1]
        field_ref[1, w] = xt[w, TH]
        live = silu(total[1 : TH - 1].reshape(inner * width, C)).reshape(inner * blocks, FC, GB, C)
        for f in range(FC):
            act[w, :, f * C : (f + 1) * C] = live[:, f].reshape(inner * half, C).astype(BF)
    wt_copy.wait()
    for w in range(TW):
        temporal = dot(act[w], temporal_matrix(wt_ref))
        field = xt[w, 2:TH].astype(F32).reshape(inner * blocks, FC, GB, C)
        for f in range(FC):
            mix[w, f] = (field[:, f].reshape(inner * half, C) + temporal[:, f * C : (f + 1) * C]).astype(BF)
    lane = lax.broadcasted_iota(jnp.int32, (GB, 4 * HALF), 1) & (HALF - 1)
    sums = [[jnp.zeros((GB, 4 * HALF), F32) for _ in range(FC)] for _ in range(blocks)]
    for w in range(TW):
        for f in range(FC):
            pixels = dot(mix[w, f], proj_ref[...])
            for h in range(inner):
                here = lane == (h + 1) * TW + w
                for b in range(blocks):
                    at = (h * blocks + b) * GB
                    sums[b][f] = jnp.where(here, pixels[at : at + GB], sums[b][f])
    for b in range(blocks):
        for f in range(FC):
            sums_ref[b, f] = sums[b][f]


def main(xt, ws, wt, wo):
    width = xt.shape[2]
    groups = width // FC
    vmem = pl.BlockSpec(memory_space=pltpu.VMEM)
    return pl.pallas_call(
        main_kernel,
        out_shape=(
            jax.ShapeDtypeStruct((2, TW, width, C), F32),
            jax.ShapeDtypeStruct((2, TW, width, C), BF),
            jax.ShapeDtypeStruct((groups // GB, FC, GB, 4 * HALF), F32),
            jax.ShapeDtypeStruct(wt.shape, BF),
            jax.ShapeDtypeStruct((C, 4 * HALF), BF),
        ),
        in_specs=[vmem, vmem, pl.BlockSpec(memory_space=pltpu.HBM), vmem],
        out_specs=(vmem,) * 5,
        scratch_shapes=[
            pltpu.VMEM((TW, (TH - 2) * groups, FC * C), BF),
            pltpu.VMEM((TW, FC, (TH - 2) * groups, C), BF),
            pltpu.SemaphoreType.DMA,
        ],
        compiler_params=pltpu.CompilerParams(vmem_limit_bytes=32 * 1024 * 1024),
        cost_estimate=pl.CostEstimate(flops=4_500_000_000, bytes_accessed=4_500_000, transcendentals=700_000),
        name="main",
    )(xt, ws, pltpu.with_memory_space_constraint(wt, pltpu.HBM), wo)


def finish_kernel(
    even_ref, live_ref, a_ref, b_ref, rim_ref, field_ref, sums_ref, proj_ref, ws_ref, wt_ref, owners_ref, out_ref
):
    blocks = sums_ref.shape[0]
    count = blocks * GB
    width = count * FC
    even = even_ref[0] == 1
    top = jnp.where(even, b_ref[...], a_ref[...])
    bottom = jnp.where(even, a_ref[...], b_ref[...])
    acts = []
    for side, (halo, dy) in enumerate(((top, 0), (bottom, 2))):
        total = rim_ref[side].reshape(TW * width, C) + dot(halo, ws_ref[dy, 1])
        left = dot(halo[: (TW - 1) * width], ws_ref[dy, 0])
        right = dot(halo[width:], ws_ref[dy, 2])
        gap = jnp.zeros((width, C), F32)
        total = total + jnp.concatenate([gap, left], axis=0) + jnp.concatenate([right, gap], axis=0)
        acts.append(silu(total).reshape(TW * blocks, FC, GB, C))
    frames = [
        jnp.concatenate([acts[side][:, f].reshape(TW * count, C) for side in range(2)], axis=0).astype(BF)
        for f in range(FC)
    ]
    temporal = dot(jnp.concatenate(frames, axis=1), temporal_matrix(wt_ref))
    field = field_ref[...].astype(F32).reshape(2 * TW * blocks, FC, GB, C)
    lane = lax.broadcasted_iota(jnp.int32, (GB, 4 * HALF), 1) & (HALF - 1)
    narrow = lax.broadcasted_iota(jnp.int32, (GB, CELLS), 1) < HALF
    sums = [[sums_ref[b, f] for f in range(FC)] for b in range(blocks)]
    for f in range(FC):
        mixed = (field[:, f].reshape(2 * TW * count, C) + temporal[:, f * C : (f + 1) * C]).astype(BF)
        pixels = dot(mixed, proj_ref[...])
        for side, h in ((0, 0), (1, TH - 1)):
            for w in range(TW):
                here = lane == h * TW + w
                for b in range(blocks):
                    at = ((side * TW + w) * blocks + b) * GB
                    sums[b][f] = jnp.where(here, pixels[at : at + GB], sums[b][f])
    channels = []
    for c in range(3):
        at = c // 2 * CELLS
        for b in range(blocks):
            first, second = sums[b][0][:, at : at + CELLS], sums[b][1][:, at : at + CELLS]
            if c % 2 == 0:
                second = pltpu.roll(second, HALF, 1)
            else:
                first = pltpu.roll(first, HALF, 1)
            channels.append(jnp.where(narrow, first, second))
    stacked = jnp.concatenate(channels, axis=0).astype(BF)
    slots = out_ref.shape[0]
    row = lax.broadcasted_iota(jnp.int32, (slots, count), 0) // 3
    group = lax.broadcasted_iota(jnp.int32, (slots, count), 1)
    streams = slots // 6
    named = jnp.broadcast_to(owners_ref[...], (slots, count)) == (row // 2 + streams // 2) % streams
    earlier = lax.broadcasted_iota(jnp.int32, (count, count), 0) < lax.broadcasted_iota(jnp.int32, (count, count), 1)
    rank = dot(named.astype(F32).astype(BF), earlier.astype(F32).astype(BF)).astype(jnp.int32)
    placed = named & (rank == row % 2) & (group < live_ref[0])
    channel = lax.broadcasted_iota(jnp.int32, (slots, count), 0) % 3
    placing = jnp.concatenate([(placed & (channel == c)).astype(F32) for c in range(3)], axis=1).astype(BF)
    message = dot(placing, stacked).astype(BF)
    out_ref[...] = message


def finish(even, live, side_a, side_b, rim, field, sums, proj, ws, wt, owners, rows):
    vmem = pl.BlockSpec(memory_space=pltpu.VMEM)
    smem = pl.BlockSpec(memory_space=pltpu.SMEM)
    return pl.pallas_call(
        finish_kernel,
        out_shape=jax.ShapeDtypeStruct((rows, CELLS), BF),
        in_specs=[smem, smem] + [vmem] * 9,
        out_specs=vmem,
        compiler_params=pltpu.CompilerParams(vmem_limit_bytes=32 * 1024 * 1024),
        cost_estimate=pl.CostEstimate(flops=500_000_000, bytes_accessed=3_000_000, transcendentals=100_000),
        name="finish",
    )(even, live, side_a, side_b, rim, field, sums, proj, ws, wt, owners)


def local(latents, owners, live_counts, spatial_weight, temporal_weight, out_weight):
    groups = latents.shape[0]
    latents = latents.reshape(groups, CELLS, C)
    streams, bands = lax.axis_size("stream"), lax.axis_size("band")
    even = (1 - (lax.axis_index("tile") & 1)).reshape(1)
    send_a, send_b, xt, ws = prep(even, latents, spatial_weight)
    side_b = lax.ppermute(send_b, "tile", [(1, 2), (2, 1)])
    side_a = lax.ppermute(send_a, "tile", [(0, 1), (1, 0), (2, 3), (3, 2)])
    rim, field, sums, wt, proj = main(xt, ws, temporal_weight, out_weight)
    rows = streams * 2 * 3
    outgoing = finish(even, live_counts, side_a, side_b, rim, field, sums, proj, ws, wt, owners.reshape(1, groups), rows)
    band_list = [6, 7, 5, 4, 3, 2, 1, 0]
    stream_list = list(range(streams // 2, streams)) + list(range(streams // 2))
    parity = lax.axis_index("band")
    signs = 1 - 2 * (lax.population_count(parity & jnp.array(band_list, dtype=jnp.int32)) & 1)
    signs = signs.astype(F32) * F32(8.0**-0.5)
    outgoing, signs = lax.optimization_barrier((outgoing.reshape(streams * 3, 2, CELLS), signs))
    got = lax.all_to_all(
        outgoing, "stream", split_axis=0, concat_axis=0, tiled=True, axis_index_groups=[stream_list]
    )
    half = streams * 3 // 2
    got = jnp.concatenate([got[half:], got[:half]], axis=0).reshape(1, rows, CELLS)
    got = lax.optimization_barrier(jnp.broadcast_to(got, (bands, rows, CELLS)))
    got = lax.all_to_all(got, "band", split_axis=0, concat_axis=0, tiled=True, axis_index_groups=[band_list])
    frames = jnp.sum(got.astype(F32) * signs[:, None, None], axis=0)
    return frames.reshape(streams * 2, 1, 3, CELLS)


def solution(mesh):
    return jax.shard_map(
        local,
        mesh=mesh,
        in_specs=(P("stream", "band", "tile", None), P("stream", None), P("stream"), P(), P(), P()),
        out_specs=P("stream", "band", None, "tile"),
        check_vma=False,
    )
```

```python
import jax
import jax.numpy as jnp
from jax import lax
from jax.experimental import pallas as pl
from jax.experimental.pallas import tpu as pltpu
from jax.sharding import PartitionSpec as P

C = 256
FC = 2
TH = 16
TW = 4
GB = 8
GF = FC * GB
CELLS = FC * TH * TW
HALF = TH * TW
BF = jnp.bfloat16
F32 = jnp.float32


def dot(a, b):
    return lax.dot_general(a, b, (((1,), (0,)), ((), ())), preferred_element_type=F32)


def silu(x):
    return 0.5 * x * (1.0 + jnp.tanh(0.5 * x))


def one_hot(rows, cols, place):
    wanted = jnp.broadcast_to(place(lax.broadcasted_iota(jnp.int32, (rows, 1), 0)), (rows, cols))
    return jnp.where(wanted == lax.broadcasted_iota(jnp.int32, (rows, cols), 1), 1.0, 0.0).astype(BF)


def temporal_matrix(wt_ref):
    first = jnp.concatenate([wt_ref[1], wt_ref[0]], axis=1)
    second = jnp.concatenate([wt_ref[2], wt_ref[1]], axis=1)
    return jnp.concatenate([first, second], axis=0)


def prep_kernel(
    even_ref, x_ref, ws_ref, a_ref, b_ref, xt_ref, ws_out, slab, sems
):
    groups = x_ref.shape[0]
    blocks = groups // GB
    width = blocks * GF
    x_copies = [
        pltpu.make_async_copy(x_ref.at[b * GB : (b + 1) * GB], slab.at[b * GB : (b + 1) * GB], sems.at[b])
        for b in range(blocks)
    ]
    ws_copy = pltpu.make_async_copy(ws_ref, ws_out, sems.at[blocks])
    for copy in x_copies + [ws_copy]:
        copy.start()
    perm = one_hot(256, 256, lambda r: (r & 7) * 32 + ((r >> 3) & 1) * 16 + ((r >> 4) & 3) * 4 + (r >> 6))
    zero_row = jnp.zeros((width, C), BF)
    for w in range(TW):
        xt_ref[w, 0] = zero_row
        xt_ref[w, TH + 1] = zero_row
    for b in range(blocks):
        x_copies[b].wait()
        for part in range(TH // 4):
            rows = jnp.concatenate(
                [
                    slab[b * GB + g, f * HALF + part * 16 : f * HALF + part * 16 + 16, :]
                    for g in range(GB)
                    for f in range(FC)
                ],
                axis=0,
            )
            moved = dot(perm, rows).astype(BF)
            for w in range(TW):
                xt_ref[w, 1 + part * 4 : 5 + part * 4, b * GF : (b + 1) * GF] = moved[w * 64 : w * 64 + 64].reshape(
                    4, GF, C
                )
    even = even_ref[0]
    for out_ref, row in ((a_ref, 1 + even * (TH - 1)), (b_ref, TH - even * (TH - 1))):
        for w in range(TW):
            out_ref[w * width : (w + 1) * width, :] = xt_ref[w, row]
    ws_copy.wait()


def prep(even, latents, ws):
    groups = latents.shape[0]
    width = groups * FC
    vmem = pl.BlockSpec(memory_space=pltpu.VMEM)
    hbm = pl.BlockSpec(memory_space=pltpu.HBM)
    return pl.pallas_call(
        prep_kernel,
        out_shape=(
            jax.ShapeDtypeStruct((TW * width, C), BF),
            jax.ShapeDtypeStruct((TW * width, C), BF),
            jax.ShapeDtypeStruct((TW, TH + 2, width, C), BF),
            jax.ShapeDtypeStruct(ws.shape, BF),
        ),
        in_specs=[pl.BlockSpec(memory_space=pltpu.SMEM)] + [hbm] * 2,
        out_specs=(vmem,) * 4,
        scratch_shapes=[
            pltpu.VMEM(latents.shape, BF),
            pltpu.SemaphoreType.DMA((groups // GB + 1,)),
        ],
        compiler_params=pltpu.CompilerParams(vmem_limit_bytes=32 * 1024 * 1024),
        cost_estimate=pl.CostEstimate(flops=400_000_000, bytes_accessed=3_200_000, transcendentals=0),
        name="prep",
    )(even, *(pltpu.with_memory_space_constraint(a, pltpu.HBM) for a in (latents, ws)))


def main_kernel(
    live_ref, xt, ws_ref, wt_hbm, wo_ref, owners_ref, rim_ref, field_ref, sums_ref, wt_ref, proj_ref, placing_ref,
    act, mix, sem,
):
    wt_copy = pltpu.make_async_copy(wt_hbm, wt_ref, sem)
    wt_copy.start()
    channel = lax.broadcasted_iota(jnp.int32, (wo_ref.shape[0], 4 * HALF), 1) // HALF
    spread = (channel == lax.broadcasted_iota(jnp.int32, channel.shape, 0)).astype(F32)
    proj_ref[...] = lax.dot_general(
        wo_ref[...].astype(F32), spread, (((0,), (0,)), ((), ())), preferred_element_type=F32
    ).astype(BF)
    width = xt.shape[2]
    blocks = width // GF
    half = blocks * GB
    slots, count = placing_ref.shape[0], half
    row = lax.broadcasted_iota(jnp.int32, (slots, count), 0) // 3
    group = lax.broadcasted_iota(jnp.int32, (slots, count), 1)
    streams = slots // 6
    named = jnp.broadcast_to(owners_ref[...], (slots, count)) == (row // 2 + streams // 2) % streams
    earlier = lax.broadcasted_iota(jnp.int32, (count, count), 0) < lax.broadcasted_iota(jnp.int32, (count, count), 1)
    rank = dot(named.astype(F32).astype(BF), earlier.astype(F32).astype(BF)).astype(jnp.int32)
    placed = named & (rank == row % 2) & (group < live_ref[0])
    channel = lax.broadcasted_iota(jnp.int32, (slots, count), 0) % 3
    placing_ref[...] = jnp.concatenate([(placed & (channel == c)).astype(F32) for c in range(3)], axis=1).astype(BF)
    inner = TH - 2
    for w in range(TW):
        taps = [(dy, dx) for dy in range(3) for dx in range(3) if 0 <= w + dx - 1 < TW]
        lhs = jnp.concatenate([xt[w + dx - 1, dy : dy + TH].reshape(TH * width, C) for dy, dx in taps], axis=1)
        rhs = jnp.concatenate([ws_ref[dy, dx] for dy, dx in taps], axis=0)
        total = dot(lhs, rhs).reshape(TH, width, C)
        rim_ref[0, w] = total[0]
        rim_ref[1, w] = total[TH - 1]
        field_ref[0, w] = xt[w, 1]
        field_ref[1, w] = xt[w, TH]
        live = silu(total[1 : TH - 1].reshape(inner * width, C)).reshape(inner * blocks, FC, GB, C)
        for f in range(FC):
            act[w, :, f * C : (f + 1) * C] = live[:, f].reshape(inner * half, C).astype(BF)
    wt_copy.wait()
    for w in range(TW):
        temporal = dot(act[w], temporal_matrix(wt_ref))
        field = xt[w, 2:TH].astype(F32).reshape(inner * blocks, FC, GB, C)
        for f in range(FC):
            mix[w, f] = (field[:, f].reshape(inner * half, C) + temporal[:, f * C : (f + 1) * C]).astype(BF)
    lane = lax.broadcasted_iota(jnp.int32, (GB, 4 * HALF), 1) & (HALF - 1)
    sums = [[jnp.zeros((GB, 4 * HALF), F32) for _ in range(FC)] for _ in range(blocks)]
    for w in range(TW):
        for f in range(FC):
            pixels = dot(mix[w, f], proj_ref[...])
            for h in range(inner):
                here = lane == (h + 1) * TW + w
                for b in range(blocks):
                    at = (h * blocks + b) * GB
                    sums[b][f] = jnp.where(here, pixels[at : at + GB], sums[b][f])
    for b in range(blocks):
        for f in range(FC):
            sums_ref[b, f] = sums[b][f]


def main(live, xt, ws, wt, wo, owners, rows):
    width = xt.shape[2]
    groups = width // FC
    vmem = pl.BlockSpec(memory_space=pltpu.VMEM)
    return pl.pallas_call(
        main_kernel,
        out_shape=(
            jax.ShapeDtypeStruct((2, TW, width, C), F32),
            jax.ShapeDtypeStruct((2, TW, width, C), BF),
            jax.ShapeDtypeStruct((groups // GB, FC, GB, 4 * HALF), F32),
            jax.ShapeDtypeStruct(wt.shape, BF),
            jax.ShapeDtypeStruct((C, 4 * HALF), BF),
            jax.ShapeDtypeStruct((rows, 3 * groups), BF),
        ),
        in_specs=[
            pl.BlockSpec(memory_space=pltpu.SMEM), vmem, vmem, pl.BlockSpec(memory_space=pltpu.HBM), vmem, vmem
        ],
        out_specs=(vmem,) * 6,
        scratch_shapes=[
            pltpu.VMEM((TW, (TH - 2) * groups, FC * C), BF),
            pltpu.VMEM((TW, FC, (TH - 2) * groups, C), BF),
            pltpu.SemaphoreType.DMA,
        ],
        compiler_params=pltpu.CompilerParams(vmem_limit_bytes=32 * 1024 * 1024),
        cost_estimate=pl.CostEstimate(flops=4_500_000_000, bytes_accessed=4_500_000, transcendentals=700_000),
        name="main",
    )(live, xt, ws, pltpu.with_memory_space_constraint(wt, pltpu.HBM), wo, owners)


def finish_kernel(
    even_ref, a_ref, b_ref, rim_ref, field_ref, sums_ref, proj_ref, ws_ref, wt_ref, placing_ref, out_ref
):
    blocks = sums_ref.shape[0]
    count = blocks * GB
    width = count * FC
    even = even_ref[0] == 1
    top = jnp.where(even, b_ref[...], a_ref[...])
    bottom = jnp.where(even, a_ref[...], b_ref[...])
    acts = []
    for side, (halo, dy) in enumerate(((top, 0), (bottom, 2))):
        total = rim_ref[side].reshape(TW * width, C) + dot(halo, ws_ref[dy, 1])
        left = dot(halo[: (TW - 1) * width], ws_ref[dy, 0])
        right = dot(halo[width:], ws_ref[dy, 2])
        gap = jnp.zeros((width, C), F32)
        total = total + jnp.concatenate([gap, left], axis=0) + jnp.concatenate([right, gap], axis=0)
        acts.append(silu(total).reshape(TW * blocks, FC, GB, C))
    frames = [
        jnp.concatenate([acts[side][:, f].reshape(TW * count, C) for side in range(2)], axis=0).astype(BF)
        for f in range(FC)
    ]
    temporal = dot(jnp.concatenate(frames, axis=1), temporal_matrix(wt_ref))
    field = field_ref[...].astype(F32).reshape(2 * TW * blocks, FC, GB, C)
    lane = lax.broadcasted_iota(jnp.int32, (GB, 4 * HALF), 1) & (HALF - 1)
    narrow = lax.broadcasted_iota(jnp.int32, (GB, CELLS), 1) < HALF
    sums = [[sums_ref[b, f] for f in range(FC)] for b in range(blocks)]
    for f in range(FC):
        mixed = (field[:, f].reshape(2 * TW * count, C) + temporal[:, f * C : (f + 1) * C]).astype(BF)
        pixels = dot(mixed, proj_ref[...])
        for side, h in ((0, 0), (1, TH - 1)):
            for w in range(TW):
                here = lane == h * TW + w
                for b in range(blocks):
                    at = ((side * TW + w) * blocks + b) * GB
                    sums[b][f] = jnp.where(here, pixels[at : at + GB], sums[b][f])
    channels = []
    for c in range(3):
        at = c // 2 * CELLS
        for b in range(blocks):
            first, second = sums[b][0][:, at : at + CELLS], sums[b][1][:, at : at + CELLS]
            if c % 2 == 0:
                second = pltpu.roll(second, HALF, 1)
            else:
                first = pltpu.roll(first, HALF, 1)
            channels.append(jnp.where(narrow, first, second))
    stacked = jnp.concatenate(channels, axis=0).astype(BF)
    out_ref[...] = dot(placing_ref[...], stacked).astype(BF)


def finish(even, side_a, side_b, rim, field, sums, proj, ws, wt, placing):
    vmem = pl.BlockSpec(memory_space=pltpu.VMEM)
    smem = pl.BlockSpec(memory_space=pltpu.SMEM)
    return pl.pallas_call(
        finish_kernel,
        out_shape=jax.ShapeDtypeStruct((placing.shape[0], CELLS), BF),
        in_specs=[smem] + [vmem] * 9,
        out_specs=vmem,
        compiler_params=pltpu.CompilerParams(vmem_limit_bytes=32 * 1024 * 1024),
        cost_estimate=pl.CostEstimate(flops=500_000_000, bytes_accessed=3_000_000, transcendentals=100_000),
        name="finish",
    )(even, side_a, side_b, rim, field, sums, proj, ws, wt, placing)


def local(latents, owners, live_counts, spatial_weight, temporal_weight, out_weight):
    groups = latents.shape[0]
    latents = latents.reshape(groups, CELLS, C)
    streams, bands = lax.axis_size("stream"), lax.axis_size("band")
    even = (1 - (lax.axis_index("tile") & 1)).reshape(1)
    send_a, send_b, xt, ws = prep(even, latents, spatial_weight)
    side_b = lax.ppermute(send_b, "tile", [(1, 2), (2, 1)])
    side_a = lax.ppermute(send_a, "tile", [(0, 1), (1, 0), (2, 3), (3, 2)])
    rows = streams * 2 * 3
    rim, field, sums, wt, proj, placing = main(
        live_counts, xt, ws, temporal_weight, out_weight, owners.reshape(1, groups), rows
    )
    outgoing = finish(even, side_a, side_b, rim, field, sums, proj, ws, wt, placing)
    band_list = [6, 7, 5, 4, 3, 2, 1, 0]
    stream_list = list(range(streams // 2, streams)) + list(range(streams // 2))
    parity = lax.axis_index("band")
    signs = 1 - 2 * (lax.population_count(parity & jnp.array(band_list, dtype=jnp.int32)) & 1)
    signs = signs.astype(F32) * F32(8.0**-0.5)
    outgoing, signs = lax.optimization_barrier((outgoing.reshape(streams * 3, 2, CELLS), signs))
    got = lax.all_to_all(
        outgoing, "stream", split_axis=0, concat_axis=0, tiled=True, axis_index_groups=[stream_list]
    )
    half = streams * 3 // 2
    got = jnp.concatenate([got[half:], got[:half]], axis=0).reshape(1, rows, CELLS)
    got = lax.optimization_barrier(jnp.broadcast_to(got, (bands, rows, CELLS)))
    got = lax.all_to_all(got, "band", split_axis=0, concat_axis=0, tiled=True, axis_index_groups=[band_list])
    frames = jnp.sum(got.astype(F32) * signs[:, None, None], axis=0)
    return frames.reshape(streams * 2, 1, 3, CELLS)


def solution(mesh):
    return jax.shard_map(
        local,
        mesh=mesh,
        in_specs=(P("stream", "band", "tile", None), P("stream", None), P("stream"), P(), P(), P()),
        out_specs=P("stream", "band", None, "tile"),
        check_vma=False,
    )
```

```python
import jax
import jax.numpy as jnp
from jax import lax
from jax.experimental import pallas as pl
from jax.experimental.pallas import tpu as pltpu
from jax.sharding import PartitionSpec as P

C = 256
FC = 2
TH = 16
TW = 4
GB = 8
GF = FC * GB
CELLS = FC * TH * TW
HALF = TH * TW
BF = jnp.bfloat16
F32 = jnp.float32


def dot(a, b):
    return lax.dot_general(a, b, (((1,), (0,)), ((), ())), preferred_element_type=F32)


def silu(x):
    return 0.5 * x * (1.0 + jnp.tanh(0.5 * x))


def one_hot(rows, cols, place):
    wanted = jnp.broadcast_to(place(lax.broadcasted_iota(jnp.int32, (rows, 1), 0)), (rows, cols))
    return jnp.where(wanted == lax.broadcasted_iota(jnp.int32, (rows, cols), 1), 1.0, 0.0).astype(BF)


def temporal_matrix(wt_ref):
    first = jnp.concatenate([wt_ref[1], wt_ref[0]], axis=1)
    second = jnp.concatenate([wt_ref[2], wt_ref[1]], axis=1)
    return jnp.concatenate([first, second], axis=0)


def prep_kernel(
    even_ref, x_ref, ws_ref, a_ref, b_ref, xt_ref, ws_out, slab, sems
):
    groups = x_ref.shape[0]
    blocks = groups // GB
    width = blocks * GF
    x_copies = [
        pltpu.make_async_copy(x_ref.at[b * GB : (b + 1) * GB], slab.at[b * GB : (b + 1) * GB], sems.at[b])
        for b in range(blocks)
    ]
    ws_copy = pltpu.make_async_copy(ws_ref, ws_out, sems.at[blocks])
    for copy in x_copies + [ws_copy]:
        copy.start()
    perm = one_hot(256, 256, lambda r: (r & 7) * 32 + ((r >> 3) & 1) * 16 + ((r >> 4) & 3) * 4 + (r >> 6))
    zero_row = jnp.zeros((width, C), BF)
    for w in range(TW):
        xt_ref[w, 0] = zero_row
        xt_ref[w, TH + 1] = zero_row
    for b in range(blocks):
        x_copies[b].wait()
        for part in range(TH // 4):
            rows = jnp.concatenate(
                [
                    slab[b * GB + g, f * HALF + part * 16 : f * HALF + part * 16 + 16, :]
                    for g in range(GB)
                    for f in range(FC)
                ],
                axis=0,
            )
            moved = dot(perm, rows).astype(BF)
            for w in range(TW):
                xt_ref[w, 1 + part * 4 : 5 + part * 4, b * GF : (b + 1) * GF] = moved[w * 64 : w * 64 + 64].reshape(
                    4, GF, C
                )
    even = even_ref[0]
    for out_ref, row in ((a_ref, 1 + even * (TH - 1)), (b_ref, TH - even * (TH - 1))):
        for w in range(TW):
            out_ref[w * width : (w + 1) * width, :] = xt_ref[w, row]
    ws_copy.wait()


def prep(even, latents, ws):
    groups = latents.shape[0]
    width = groups * FC
    vmem = pl.BlockSpec(memory_space=pltpu.VMEM)
    hbm = pl.BlockSpec(memory_space=pltpu.HBM)
    return pl.pallas_call(
        prep_kernel,
        out_shape=(
            jax.ShapeDtypeStruct((TW * width, C), BF),
            jax.ShapeDtypeStruct((TW * width, C), BF),
            jax.ShapeDtypeStruct((TW, TH + 2, width, C), BF),
            jax.ShapeDtypeStruct(ws.shape, BF),
        ),
        in_specs=[pl.BlockSpec(memory_space=pltpu.SMEM)] + [hbm] * 2,
        out_specs=(vmem,) * 4,
        scratch_shapes=[
            pltpu.VMEM(latents.shape, BF),
            pltpu.SemaphoreType.DMA((groups // GB + 1,)),
        ],
        compiler_params=pltpu.CompilerParams(vmem_limit_bytes=32 * 1024 * 1024),
        cost_estimate=pl.CostEstimate(flops=400_000_000, bytes_accessed=3_200_000, transcendentals=0),
        name="prep",
    )(even, *(pltpu.with_memory_space_constraint(a, pltpu.HBM) for a in (latents, ws)))


def main_kernel(
    live_ref, xt, ws_ref, wt_hbm, wo_ref, owners_ref, rim_ref, field_ref, sums_ref, wt_ref, proj_ref, placing_ref,
    act, mix, sem,
):
    wt_copy = pltpu.make_async_copy(wt_hbm, wt_ref, sem)
    wt_copy.start()
    channel = lax.broadcasted_iota(jnp.int32, (wo_ref.shape[0], 4 * HALF), 1) // HALF
    spread = (channel == lax.broadcasted_iota(jnp.int32, channel.shape, 0)).astype(F32)
    proj_ref[...] = lax.dot_general(
        wo_ref[...].astype(F32), spread, (((0,), (0,)), ((), ())), preferred_element_type=F32
    ).astype(BF)
    width = xt.shape[2]
    blocks = width // GF
    half = blocks * GB
    slots, count = placing_ref.shape[0], half
    row = lax.broadcasted_iota(jnp.int32, (slots, count), 0) // 3
    group = lax.broadcasted_iota(jnp.int32, (slots, count), 1)
    streams = slots // 6
    named = jnp.broadcast_to(owners_ref[...], (slots, count)) == (row // 2 + streams // 2) % streams
    earlier = lax.broadcasted_iota(jnp.int32, (count, count), 0) < lax.broadcasted_iota(jnp.int32, (count, count), 1)
    rank = dot(named.astype(F32).astype(BF), earlier.astype(F32).astype(BF)).astype(jnp.int32)
    placed = named & (rank == row % 2) & (group < live_ref[0])
    channel = lax.broadcasted_iota(jnp.int32, (slots, count), 0) % 3
    placing_ref[...] = jnp.concatenate([(placed & (channel == c)).astype(F32) for c in range(3)], axis=1).astype(BF)
    inner = TH - 2
    for w in range(TW):
        taps = [(dy, dx) for dy in range(3) for dx in range(3) if 0 <= w + dx - 1 < TW]
        lhs = jnp.concatenate([xt[w + dx - 1, dy : dy + TH].reshape(TH * width, C) for dy, dx in taps], axis=1)
        rhs = jnp.concatenate([ws_ref[dy, dx] for dy, dx in taps], axis=0)
        total = dot(lhs, rhs).reshape(TH, width, C)
        rim_ref[0, w] = total[0]
        rim_ref[1, w] = total[TH - 1]
        field_ref[0, w] = xt[w, 1]
        field_ref[1, w] = xt[w, TH]
        live = silu(total[1 : TH - 1].reshape(inner * width, C)).reshape(inner * blocks, FC, GB, C)
        for f in range(FC):
            act[w, :, f * C : (f + 1) * C] = live[:, f].reshape(inner * half, C).astype(BF)
    wt_copy.wait()
    for w in range(TW):
        temporal = dot(act[w], temporal_matrix(wt_ref))
        field = xt[w, 2:TH].astype(F32).reshape(inner * blocks, FC, GB, C)
        for f in range(FC):
            mix[w, f] = (field[:, f].reshape(inner * half, C) + temporal[:, f * C : (f + 1) * C]).astype(BF)
    lane = lax.broadcasted_iota(jnp.int32, (GB, 4 * HALF), 1) & (HALF - 1)
    sums = [[jnp.zeros((GB, 4 * HALF), F32) for _ in range(FC)] for _ in range(blocks)]
    for w in range(TW):
        for f in range(FC):
            pixels = dot(mix[w, f], proj_ref[...])
            for h in range(inner):
                here = lane == (h + 1) * TW + w
                for b in range(blocks):
                    at = (h * blocks + b) * GB
                    sums[b][f] = jnp.where(here, pixels[at : at + GB], sums[b][f])
    for b in range(blocks):
        for f in range(FC):
            sums_ref[b, f] = sums[b][f]


def main(live, xt, ws, wt, wo, owners, rows):
    width = xt.shape[2]
    groups = width // FC
    vmem = pl.BlockSpec(memory_space=pltpu.VMEM)
    return pl.pallas_call(
        main_kernel,
        out_shape=(
            jax.ShapeDtypeStruct((2, TW, width, C), F32),
            jax.ShapeDtypeStruct((2, TW, width, C), BF),
            jax.ShapeDtypeStruct((groups // GB, FC, GB, 4 * HALF), F32),
            jax.ShapeDtypeStruct(wt.shape, BF),
            jax.ShapeDtypeStruct((C, 4 * HALF), BF),
            jax.ShapeDtypeStruct((rows, 3 * groups), BF),
        ),
        in_specs=[
            pl.BlockSpec(memory_space=pltpu.SMEM), vmem, vmem, pl.BlockSpec(memory_space=pltpu.HBM), vmem, vmem
        ],
        out_specs=(vmem,) * 6,
        scratch_shapes=[
            pltpu.VMEM((TW, (TH - 2) * groups, FC * C), BF),
            pltpu.VMEM((TW, FC, (TH - 2) * groups, C), BF),
            pltpu.SemaphoreType.DMA,
        ],
        compiler_params=pltpu.CompilerParams(vmem_limit_bytes=32 * 1024 * 1024),
        cost_estimate=pl.CostEstimate(flops=4_500_000_000, bytes_accessed=4_500_000, transcendentals=700_000),
        name="main",
    )(live, xt, ws, pltpu.with_memory_space_constraint(wt, pltpu.HBM), wo, owners)


def finish_kernel(
    even_ref, a_ref, b_ref, rim_ref, field_ref, sums_ref, proj_ref, ws_ref, wt_ref, placing_ref, out_ref
):
    blocks = sums_ref.shape[0]
    count = blocks * GB
    width = count * FC
    even = even_ref[0] == 1
    top = jnp.where(even, b_ref[...], a_ref[...])
    bottom = jnp.where(even, a_ref[...], b_ref[...])
    acts = []
    for side, (halo, dy) in enumerate(((top, 0), (bottom, 2))):
        total = rim_ref[side].reshape(TW * width, C) + dot(halo, ws_ref[dy, 1])
        left = dot(halo[: (TW - 1) * width], ws_ref[dy, 0])
        right = dot(halo[width:], ws_ref[dy, 2])
        gap = jnp.zeros((width, C), F32)
        total = total + jnp.concatenate([gap, left], axis=0) + jnp.concatenate([right, gap], axis=0)
        acts.append(silu(total).reshape(TW * blocks, FC, GB, C))
    frames = [
        jnp.concatenate([acts[side][:, f].reshape(TW * count, C) for side in range(2)], axis=0).astype(BF)
        for f in range(FC)
    ]
    temporal = dot(jnp.concatenate(frames, axis=1), temporal_matrix(wt_ref))
    field = field_ref[...].astype(F32).reshape(2 * TW * blocks, FC, GB, C)
    lane = lax.broadcasted_iota(jnp.int32, (GB, 4 * HALF), 1) & (HALF - 1)
    narrow = lax.broadcasted_iota(jnp.int32, (GB, CELLS), 1) < HALF
    sums = [[sums_ref[b, f] for f in range(FC)] for b in range(blocks)]
    for f in range(FC):
        mixed = (field[:, f].reshape(2 * TW * count, C) + temporal[:, f * C : (f + 1) * C]).astype(BF)
        pixels = dot(mixed, proj_ref[...])
        for side, h in ((0, 0), (1, TH - 1)):
            for w in range(TW):
                here = lane == h * TW + w
                for b in range(blocks):
                    at = ((side * TW + w) * blocks + b) * GB
                    sums[b][f] = jnp.where(here, pixels[at : at + GB], sums[b][f])
    channels = []
    for c in range(3):
        at = c // 2 * CELLS
        for b in range(blocks):
            first, second = sums[b][0][:, at : at + CELLS], sums[b][1][:, at : at + CELLS]
            if c % 2 == 0:
                second = pltpu.roll(second, HALF, 1)
            else:
                first = pltpu.roll(first, HALF, 1)
            channels.append(jnp.where(narrow, first, second))
    stacked = jnp.concatenate(channels, axis=0).astype(BF)
    out_ref[...] = dot(placing_ref[...], stacked).astype(BF)


def finish(even, side_a, side_b, rim, field, sums, proj, ws, wt, placing):
    vmem = pl.BlockSpec(memory_space=pltpu.VMEM)
    smem = pl.BlockSpec(memory_space=pltpu.SMEM)
    return pl.pallas_call(
        finish_kernel,
        out_shape=jax.ShapeDtypeStruct((placing.shape[0], CELLS), BF),
        in_specs=[smem] + [vmem] * 9,
        out_specs=vmem,
        compiler_params=pltpu.CompilerParams(vmem_limit_bytes=32 * 1024 * 1024),
        cost_estimate=pl.CostEstimate(flops=500_000_000, bytes_accessed=3_000_000, transcendentals=100_000),
        name="finish",
    )(even, side_a, side_b, rim, field, sums, proj, ws, wt, placing)


def local(latents, owners, live_counts, spatial_weight, temporal_weight, out_weight):
    groups = latents.shape[0]
    latents = latents.reshape(groups, CELLS, C)
    streams, bands = lax.axis_size("stream"), lax.axis_size("band")
    even = (1 - (lax.axis_index("tile") & 1)).reshape(1)
    send_a, send_b, xt, ws = prep(even, latents, spatial_weight)
    side_b = lax.ppermute(send_b, "tile", [(1, 2), (2, 1)])
    side_a = lax.ppermute(send_a, "tile", [(0, 1), (1, 0), (2, 3), (3, 2)])
    rows = streams * 2 * 3
    rim, field, sums, wt, proj, placing = main(
        live_counts, xt, ws, temporal_weight, out_weight, owners.reshape(1, groups), rows
    )
    outgoing = finish(even, side_a, side_b, rim, field, sums, proj, ws, wt, placing)
    band_list = [6, 7, 5, 4, 3, 2, 1, 0]
    stream_list = list(range(streams // 2, streams)) + list(range(streams // 2))
    parity = lax.axis_index("band")
    signs = 1 - 2 * (lax.population_count(parity & jnp.array(band_list, dtype=jnp.int32)) & 1)
    signs = signs.astype(F32) * F32(8.0**-0.5)
    outgoing, signs = lax.optimization_barrier((outgoing.reshape(streams * 3, 2, CELLS), signs))
    got = lax.all_to_all(
        outgoing, "stream", split_axis=0, concat_axis=0, tiled=True, axis_index_groups=[stream_list]
    )
    got = lax.optimization_barrier(jnp.broadcast_to(got.reshape(1, rows, CELLS), (bands, rows, CELLS)))
    got = lax.all_to_all(got, "band", split_axis=0, concat_axis=0, tiled=True, axis_index_groups=[band_list])
    got = got.reshape(bands, 2, rows // 2, CELLS)[:, ::-1].astype(F32)
    frames = jnp.sum(got * signs[:, None, None, None], axis=0)
    return frames.reshape(streams * 2, 1, 3, CELLS)


def solution(mesh):
    return jax.shard_map(
        local,
        mesh=mesh,
        in_specs=(P("stream", "band", "tile", None), P("stream", None), P("stream"), P(), P(), P()),
        out_specs=P("stream", "band", None, "tile"),
        check_vma=False,
    )
```
